32 devices in a mesh: groups: 2 (over x), ctx: 16 (over z, y, core).
Axes of the slice: x: 2, y: 2, z: 4, core: 2. Of those that a mesh axis runs over, the one named last changes fastest.
Arguments:
- queries: bfloat16 [6144, 4096], P(('groups', 'ctx')), parts along dimension 0, may hold values from -6 to 6
- keys: bfloat16 [6144, 1024], P(('groups', 'ctx')), parts along dimension 0, may hold values from -6 to 6
- values: bfloat16 [6144, 1024], P(('groups', 'ctx')), parts along dimension 0, may hold values from -6 to 6
- grad_out: bfloat16 [6144, 4096], P(('groups', 'ctx')), parts along dimension 0, may hold values from -6 to 6
- positions: int32 [6144], P('groups'), parts along dimension 0, may hold values from 0 to 3071, as said below
- segments: int32 [6144], P('groups'), parts along dimension 0, may hold values from 0 to 1, as said below
Outputs:
- grad_queries: bfloat16 [6144, 4096], P(('groups', 'ctx')), parts along dimension 0
- grad_keys: bfloat16 [6144, 1024], P(('groups', 'ctx')), parts along dimension 0
- grad_values: bfloat16 [6144, 1024], P(('groups', 'ctx')), parts along dimension 0
The draws below stay inside these ranges and needn't reach their ends.
There are 2 independent parts, one for each index of `groups`. The reference program is written for one: setup_inputs(seed, part) draws one part's arguments, and reference() takes and returns one part's arrays. A program takes and returns all parts, laid end to end along the dimension named above; each array names one. Nothing has to cross between parts.
Inputs may be any that keep to these rules, and one draw needn't show every extreme that they name: Rows b * 192 to (b + 1) * 192 - 1 hold the positions b * 192 to (b + 1) * 192 - 1, each once, in some order. `segments`: document ids never fall as positions rise; two tokens are in the same document exactly when their ids are equal. Each aligned run of 1536 positions holds exactly one document start, the first at position 0.
All inputs are finite; a program needn't handle non-finite values.
Results may differ from the reference program's by a relative error of at most 0.0087.
Values may be sent and summed in bfloat16 or wider, within the bound.
A program may use at most 128 MiB of HBM per device.

```python
import jax
import jax.numpy as jnp
from jax import lax

HQ = 32
HK = 8
DH = 128
TOK_DEV = 192
WINDOW = 768
TOKENS = 3072


def block_positions(key):
    inner = jax.random.fold_in(key, 11)
    nblocks = TOKENS // TOK_DEV
    ranks = jax.random.randint(inner, (nblocks, TOK_DEV), 0, 1 << 20) * TOK_DEV + jnp.arange(TOK_DEV, dtype=jnp.int32)[None, :]
    order = jnp.argsort(ranks, axis=1).astype(jnp.int32)
    return (order + (jnp.arange(nblocks, dtype=jnp.int32) * TOK_DEV)[:, None]).reshape(-1).astype(jnp.int32)


def draw_positions(key, part):
    return block_positions(key)


def draw_segments(key, part):
    stored = block_positions(key)
    key = jax.random.fold_in(key, 12)
    run_len = 8 * TOK_DEV
    nruns = TOKENS // run_len
    offsets = jax.random.randint(key, (nruns,), 0, run_len).astype(jnp.int32)
    offsets = jnp.where(jnp.arange(nruns) == 0, 0, offsets).astype(jnp.int32)
    where = jnp.arange(TOKENS, dtype=jnp.int32)
    starts = (where % run_len == offsets[where // run_len]).astype(jnp.int32)
    by_position = (jnp.cumsum(starts) - 1).astype(jnp.int32)
    return by_position[stored]


def draw_queries(key, part):
    key = jax.random.fold_in(key, 1)
    base = jnp.clip(jax.random.normal(key, (TOKENS, HQ, DH), jnp.float32), -6.0, 6.0)
    return base.reshape(TOKENS, HQ * DH).astype(jnp.bfloat16)


def draw_keys(key, part):
    key = jax.random.fold_in(key, 2)
    base = jnp.clip(jax.random.normal(key, (TOKENS, HK, DH), jnp.float32), -6.0, 6.0)
    return base.reshape(TOKENS, HK * DH).astype(jnp.bfloat16)


def block_scale(key, dims, pieces, least, high):
    factor_of, own = 1.0, jax.random.fold_in(key, 6)
    for position, parts in pieces:
        steps = jnp.exp(jax.random.uniform(jax.random.fold_in(own, position), (parts,), jnp.float32, least / len(pieces), high / len(pieces)))
        factor_of = factor_of * jnp.repeat(steps, dims[position] // parts).reshape([-1 if axis == position else 1 for axis in range(len(dims))])
    return factor_of


def gaussian(stream_key, shape, width, bound, shards=(), kind=jnp.bfloat16):
    loudness = block_scale(stream_key, shape, shards, -0.22, 0.18) if shards else 1.0
    entries = jax.random.normal(stream_key, shape, jnp.float32) * width * loudness
    return jnp.minimum(jnp.maximum(entries, -bound), bound).astype(kind)


def setup_inputs(seed: int = 0, part: int = 0) -> dict:
    arg_keys = jax.random.split(jax.random.key(seed), 7)
    part_keys = jax.random.split(jax.random.fold_in(arg_keys[6], part), 7)
    return {
        "queries": draw_queries(jax.random.fold_in(jax.random.fold_in(arg_keys[6], part), 71), part),
        "keys": draw_keys(jax.random.fold_in(jax.random.fold_in(arg_keys[6], part), 71), part),
        "values": gaussian(part_keys[2], (TOKENS, HK * DH), 1.0, 6.0, ((0, 16),)),
        "grad_out": gaussian(part_keys[3], (TOKENS, HQ * DH), 1.0, 6.0, ((0, 16),)),
        "positions": draw_positions(jax.random.fold_in(jax.random.fold_in(arg_keys[6], part), 71), part),
        "segments": draw_segments(jax.random.fold_in(jax.random.fold_in(arg_keys[6], part), 71), part),
    }


def block_grads(query_blk, key_blk, value_blk, grad_blk, mask):
    scale = float(DH) ** -0.5
    scores = jnp.einsum("tkgd,skd->kgts", query_blk, key_blk) * scale
    masked = jnp.where(mask[None, None], scores, -jnp.inf)
    row_max = jnp.max(masked, -1, keepdims=True)
    lse = row_max + jnp.log(jnp.sum(jnp.exp(masked - row_max), -1, keepdims=True))
    probs = jnp.where(mask[None, None], jnp.exp(masked - lse), jnp.float32(0.0))
    probs_low = lax.optimization_barrier(probs.astype(jnp.bfloat16)).astype(jnp.float32)
    output = jnp.einsum("kgts,skd->tkgd", probs_low, value_blk)
    delta = jnp.transpose(jnp.sum(grad_blk * output, -1), (1, 2, 0))
    dprob = jnp.einsum("tkgd,skd->kgts", grad_blk, value_blk)
    dscore = probs * (dprob - delta[..., None]) * scale
    dscore = lax.optimization_barrier(dscore.astype(jnp.bfloat16)).astype(jnp.float32)
    grad_query = jnp.einsum("kgts,skd->tkgd", dscore, key_blk)
    grad_key = jnp.einsum("kgts,tkgd->skd", dscore, query_blk)
    grad_value = jnp.einsum("kgts,tkgd->skd", probs_low, grad_blk)
    return grad_query, grad_key, grad_value


def reference(queries, keys, values, grad_out, positions, segments):
    span = 5 * TOK_DEV
    margin = 4 * TOK_DEV
    group_size = HQ // HK
    nblocks = TOKENS // TOK_DEV
    key_pad = jnp.concatenate([jnp.zeros((margin, HK * DH), jnp.bfloat16), keys]).reshape(-1, HK, DH)
    value_pad = jnp.concatenate([jnp.zeros((margin, HK * DH), jnp.bfloat16), values]).reshape(-1, HK, DH)
    pos_pad = jnp.concatenate([jnp.zeros((margin,), jnp.int32), positions])
    seg_pad = jnp.concatenate([jnp.full((margin,), -1, jnp.int32), segments])
    zero_index = jnp.zeros((), jnp.int32)

    def visit(carry, block):
        key_acc, value_acc = carry
        start = (block * TOK_DEV).astype(jnp.int32)
        query_blk = lax.dynamic_slice_in_dim(queries, start, TOK_DEV, 0).reshape(TOK_DEV, HK, group_size, DH).astype(jnp.float32)
        grad_blk = lax.dynamic_slice_in_dim(grad_out, start, TOK_DEV, 0).reshape(TOK_DEV, HK, group_size, DH).astype(jnp.float32)
        query_pos = lax.dynamic_slice_in_dim(positions, start, TOK_DEV, 0)
        query_seg = lax.dynamic_slice_in_dim(segments, start, TOK_DEV, 0)
        key_blk = lax.dynamic_slice_in_dim(key_pad, start, span, 0).astype(jnp.float32)
        value_blk = lax.dynamic_slice_in_dim(value_pad, start, span, 0).astype(jnp.float32)
        key_pos = lax.dynamic_slice_in_dim(pos_pad, start, span, 0)
        key_seg = lax.dynamic_slice_in_dim(seg_pad, start, span, 0)
        mask = (query_seg[:, None] == key_seg[None, :]) & (key_pos[None, :] <= query_pos[:, None]) & (query_pos[:, None] - key_pos[None, :] < WINDOW)
        grad_query, grad_key, grad_value = block_grads(query_blk, key_blk, value_blk, grad_blk, mask)
        index = (start, zero_index, zero_index)
        key_acc = lax.dynamic_update_slice(key_acc, lax.dynamic_slice(key_acc, index, (span, HK, DH)) + grad_key, index)
        value_acc = lax.dynamic_update_slice(value_acc, lax.dynamic_slice(value_acc, index, (span, HK, DH)) + grad_value, index)
        return (key_acc, value_acc), grad_query.reshape(TOK_DEV, HQ * DH).astype(jnp.bfloat16)

    initial = (jnp.zeros((TOKENS + margin, HK, DH), jnp.float32), jnp.zeros((TOKENS + margin, HK, DH), jnp.float32))
    (key_acc, value_acc), grad_blocks = lax.scan(visit, initial, jnp.arange(nblocks, dtype=jnp.int32))
    grad_queries = grad_blocks.reshape(TOKENS, HQ * DH)
    grad_keys = key_acc[margin:].reshape(TOKENS, HK * DH).astype(jnp.bfloat16)
    grad_values = value_acc[margin:].reshape(TOKENS, HK * DH).astype(jnp.bfloat16)
    return (grad_queries, grad_keys, grad_values)
```

```python
import functools

import jax
import jax.numpy as jnp
from jax import lax
from jax.experimental import pallas as pl
from jax.experimental.pallas import tpu as pltpu
from jax.sharding import PartitionSpec as P

HQ = 32
HK = 8
DH = 128
GROUP = HQ // HK
WINDOW = 768
HALO = 4
SCALE = float(DH) ** (-0.5)
LOG2E = 1.4426950408889634
NEG = -1e30
NT = (((1,), (1,)), ((), ()))
TN = (((0,), (0,)), ((), ()))
NN = (((1,), (0,)), ((), ()))


def dot(a, b, dims):
    return lax.dot_general(a, b, dims, preferred_element_type=jnp.float32)


def tile_grads(k, v, q, do, bias):
    s = dot(k, q, NT) + bias
    dp = dot(v, do, NT)
    m = jnp.max(s, axis=0, keepdims=True)
    e = jnp.exp2((s - m) * (SCALE * LOG2E))
    inv = 1.0 / jnp.sum(e, axis=0, keepdims=True)
    delta = jnp.sum(e * dp, axis=0, keepdims=True) * inv
    p = (e * inv).astype(jnp.bfloat16)
    a = inv * SCALE
    ds = (e * (dp * a - delta * a)).astype(jnp.bfloat16)
    dv = dot(p, do, NN)
    dk = dot(ds, q, NN)
    dq = dot(ds, k, TN)
    return dq, dk, dv


CHUNK = 256


def kernel(q_ref, do_ref, k_ref, v_ref, bias_ref, dq_ref, dk_ref, dv_ref, bias4):
    tok = q_ref.shape[0]

    @pl.when(pl.program_id(0) == 0)
    def _():
        b = bias_ref[...]
        bias4[...] = jnp.concatenate([b] * GROUP, axis=1)

    k = k_ref[...]
    v = v_ref[...]
    q = jnp.concatenate([q_ref[:, g * DH:(g + 1) * DH] for g in range(GROUP)], axis=0)
    do = jnp.concatenate([do_ref[:, g * DH:(g + 1) * DH] for g in range(GROUP)], axis=0)
    dqs = []
    dk = dv = None
    for c in range(GROUP * tok // CHUNK):
        cut = slice(c * CHUNK, (c + 1) * CHUNK)
        dq, dk1, dv1 = tile_grads(k, v, q[cut], do[cut], bias4[:, cut])
        dqs.append(dq.astype(jnp.bfloat16))
        dk = dk1 if dk is None else dk + dk1
        dv = dv1 if dv is None else dv + dv1
    dq = jnp.concatenate(dqs, axis=0)
    for g in range(GROUP):
        dq_ref[:, g * DH:(g + 1) * DH] = dq[g * tok:(g + 1) * tok]
    dk_ref[...] = dk.astype(jnp.bfloat16)
    dv_ref[...] = dv.astype(jnp.bfloat16)


def shift(x, distance):
    n = lax.axis_size("ctx")
    route = [(i, i + distance) for i in range(n) if 0 <= i + distance < n]
    return lax.ppermute(x, "ctx", route)


def per_device(queries, keys, values, grad_out, positions, segments):
    tok = queries.shape[0]
    me = lax.axis_index("ctx")
    span = (HALO + 1) * tok
    kv = jnp.concatenate([keys, values], axis=1)
    kv_all = jnp.concatenate([shift(kv, d) for d in range(HALO, 0, -1)] + [kv], axis=0)
    pos_pad = jnp.concatenate([jnp.full((HALO * tok,), -1, jnp.int32), positions])
    seg_pad = jnp.concatenate([jnp.full((HALO * tok,), -1, jnp.int32), segments])
    kpos = lax.dynamic_slice_in_dim(pos_pad, me * tok, span)[:, None]
    kseg = lax.dynamic_slice_in_dim(seg_pad, me * tok, span)[:, None]
    qpos = lax.dynamic_slice_in_dim(positions, me * tok, tok)[None, :]
    qseg = lax.dynamic_slice_in_dim(segments, me * tok, tok)[None, :]
    mask = (kseg == qseg) & (kpos <= qpos) & (qpos - kpos < WINDOW)
    bias = jnp.where(mask, 0.0, NEG).astype(jnp.float32)
    kd = HK * DH
    dq, dk, dv = pl.pallas_call(
        kernel,
        grid=(HK,),
        in_specs=[
            pl.BlockSpec((tok, GROUP * DH), lambda h: (0, h)),
            pl.BlockSpec((tok, GROUP * DH), lambda h: (0, h)),
            pl.BlockSpec((span, DH), lambda h: (0, h)),
            pl.BlockSpec((span, DH), lambda h: (0, h + HK)),
            pl.BlockSpec((span, tok), lambda h: (0, 0)),
        ],
        out_specs=[
            pl.BlockSpec((tok, GROUP * DH), lambda h: (0, h)),
            pl.BlockSpec((span, DH), lambda h: (0, h)),
            pl.BlockSpec((span, DH), lambda h: (0, h)),
        ],
        out_shape=[
            jax.ShapeDtypeStruct((tok, HQ * DH), jnp.bfloat16),
            jax.ShapeDtypeStruct((span, kd), jnp.bfloat16),
            jax.ShapeDtypeStruct((span, kd), jnp.bfloat16),
        ],
        scratch_shapes=[pltpu.VMEM((span, GROUP * tok), jnp.float32)],
        compiler_params=pltpu.CompilerParams(vmem_limit_bytes=48 * 1024 * 1024),
    )(queries, grad_out, kv_all, kv_all, bias)
    own = jnp.stack([dk[HALO * tok:], dv[HALO * tok:]]).astype(jnp.float32)
    for d in range(1, HALO + 1):
        lo = (HALO - d) * tok
        part = jnp.stack([dk[lo:lo + tok], dv[lo:lo + tok]])
        own = own + shift(part, -d).astype(jnp.float32)
    own = own.astype(jnp.bfloat16)
    return dq, own[0], own[1]


def solution(mesh):
    rows = P(("groups", "ctx"), None)
    return jax.shard_map(
        per_device,
        mesh=mesh,
        in_specs=(rows, rows, rows, rows, P("groups"), P("groups")),
        out_specs=(rows, rows, rows),
        check_vma=False,
    )
```

```python
import functools

import jax
import jax.numpy as jnp
from jax import lax
from jax.experimental import pallas as pl
from jax.experimental.pallas import tpu as pltpu
from jax.sharding import PartitionSpec as P

HQ = 32
HK = 8
DH = 128
GROUP = HQ // HK
WINDOW = 768
HALO = 4
SCALE = float(DH) ** (-0.5)
LOG2E = 1.4426950408889634
NEG = -1e30
SHIFT = 1 << 20
CHUNK = 256
NT = (((1,), (1,)), ((), ()))
TN = (((0,), (0,)), ((), ()))
NN = (((1,), (0,)), ((), ()))


def dot(a, b, dims):
    return lax.dot_general(a, b, dims, preferred_element_type=jnp.float32)


def tile_grads(k, v, q, do, bias):
    s = dot(k, q, NT) + bias
    dp = dot(v, do, NT)
    m = jnp.max(s, axis=0, keepdims=True)
    e = jnp.exp2((s - m) * (SCALE * LOG2E))
    inv = 1.0 / jnp.sum(e, axis=0, keepdims=True)
    delta = jnp.sum(e * dp, axis=0, keepdims=True) * inv
    p = (e * inv).astype(jnp.bfloat16)
    a = inv * SCALE
    ds = (e * (dp * a - delta * a)).astype(jnp.bfloat16)
    dv = dot(p, do, NN)
    dk = dot(ds, q, NN)
    dq = dot(ds, k, TN)
    return dq, dk, dv


def remote(src, dst, send, recv, device):
    return pltpu.make_async_remote_copy(
        src_ref=src,
        dst_ref=dst,
        send_sem=send,
        recv_sem=recv,
        device_id={"ctx": device},
        device_id_type=pl.DeviceIdType.MESH,
    )


def kernel(
    n, q_in, do_in, k_in, v_in, code_ref,
    dq_out, dk_out, dv_out,
    qd, kv, dqb, part, back, peer, acc_k, acc_v, bias,
    loc_sem, qd_send, qd_recv, kv_send, kv_recv, dq_sem, ret_send, ret_recv, peer_recv,
):
    tok = q_in.shape[0]
    heads = HK // 2
    wide = GROUP * DH
    span = (HALO + 1) * tok
    me = lax.axis_index("ctx")
    core = lax.rem(me, 2)
    chip = me // 2
    chips = n // 2
    mate = me + 1 - 2 * core
    other = 1 - core
    sides = (-2, -1, 1, 2)

    def dev(delta, c):
        return (chip + delta) * 2 + c

    def have(delta):
        return (chip + delta >= 0) & (chip + delta < chips)

    def cols(base, j, width):
        return pl.ds(pl.multiple_of((base * heads + j) * width, width), width)

    def rows(block):
        return pl.ds(pl.multiple_of(block * tok, 64), tok)

    barrier = pltpu.get_barrier_semaphore()
    pl.semaphore_signal(barrier, inc=1, device_id={"ctx": mate}, device_id_type=pl.DeviceIdType.MESH)
    for delta in sides:
        @pl.when(have(delta))
        def _(delta=delta):
            for c in range(2):
                pl.semaphore_signal(
                    barrier, inc=1, device_id={"ctx": dev(delta, c)}, device_id_type=pl.DeviceIdType.MESH
                )
    amount = 1 + 2 * (jnp.minimum(chip, 2) + jnp.minimum(chips - 1 - chip, 2))
    pl.semaphore_wait(barrier, amount)

    srcs = ((q_in, do_in), (k_in, v_in))

    def local_copies(j):
        out = []
        for a in range(2):
            out.append(pltpu.make_async_copy(
                srcs[0][a].at[:, cols(core, j, wide)], qd.at[j, a, core], loc_sem.at[j, a]))
            out.append(pltpu.make_async_copy(
                srcs[1][a].at[:, cols(core, j, DH)], kv.at[j, a, rows(HALO + core)], loc_sem.at[j, 2 + a]))
        return out

    def q_copy(j, a):
        return remote(srcs[0][a].at[:, cols(other, j, wide)], qd.at[j, a, core],
                      qd_send.at[j, a], qd_recv.at[j, a], mate)

    def q_arrival(j, a):
        return remote(srcs[0][a].at[:, cols(other, j, wide)], qd.at[j, a, other],
                      qd_send.at[j, a], qd_recv.at[j, a], mate)

    def kv_copy(j, a, delta, c):
        return remote(srcs[1][a].at[:, cols(c, j, DH)], kv.at[j, a, rows(HALO - 2 * delta + core)],
                      kv_send.at[j, a, 2 * delta + c], kv_recv.at[j, a, HALO - 2 * delta + core], dev(delta, c))

    def kv_arrival(j, a, block, c):
        return remote(srcs[1][a].at[:, cols(core, j, DH)], kv.at[j, a, rows(block)],
                      kv_send.at[j, a, 0], kv_recv.at[j, a, block], mate)

    @pl.loop(0, heads)
    def _(j):
        for delta in (2, 1):
            @pl.when(have(delta))
            def _(delta=delta):
                for c in range(2):
                    for a in range(2):
                        kv_copy(j, a, delta, c).start()
        for a in range(2):
            kv_copy(j, a, 0, other).start()
            q_copy(j, a).start()
        for copy in local_copies(j):
            copy.start()

    for delta in (1, 2):
        @pl.when(jnp.logical_not(have(-delta)))
        def _(delta=delta):
            lo = (HALO - 2 * delta) * tok
            kv[:, :, lo:lo + 2 * tok, :] = jnp.zeros((heads, 2, 2 * tok, DH), kv.dtype)

        @pl.when(jnp.logical_not(have(delta)))
        def _(delta=delta):
            back[delta - 1] = jnp.zeros(back.shape[1:], back.dtype)

    start = pl.multiple_of(chip * (2 * tok), 128)
    code = code_ref[:, pl.ds(start, span + tok)]
    column = jnp.broadcast_to(code, (8, span + tok)).T[:, 0:1]
    for b in range(2):
        lo = (HALO + b) * tok
        row = jnp.concatenate([code[:, lo:lo + tok]] * GROUP, axis=1)
        gap = row - column[b * tok:b * tok + span]
        bias[b] = jnp.where((gap >= 0) & (gap < WINDOW), 0.0, NEG).astype(jnp.float32)

    def ret_copy(j, block):
        delta = HALO // 2 - block // 2
        return remote(part.at[j, :, block * tok:(block + 1) * tok], back.at[delta - 1, core, j],
                      ret_send.at[j, block], ret_recv.at[j, delta - 1, core], dev(-delta, block % 2))

    def ret_arrival(j, delta, c):
        return remote(part.at[j, :, 0:tok], back.at[delta - 1, c, j],
                      ret_send.at[j, 0], ret_recv.at[j, delta - 1, c], mate)

    def peer_copy(j):
        return remote(part.at[j, :, rows(HALO + other)], peer.at[j],
                      ret_send.at[j, HALO], peer_recv.at[j], mate)

    def dq_copy(j):
        return remote(dqb.at[j, other], dq_out.at[:, cols(core, j, wide)],
                      dq_sem.at[j, 0], dq_sem.at[j, 1], mate)

    def dq_arrival(j):
        return remote(dqb.at[j, other], dq_out.at[:, cols(other, j, wide)],
                      dq_sem.at[j, 0], dq_sem.at[j, 1], mate)

    def dq_keep(j):
        return pltpu.make_async_copy(dqb.at[j, core], dq_out.at[:, cols(core, j, wide)], dq_sem.at[j, 2])

    @pl.loop(0, heads)
    def _(j):
        for copy in local_copies(j):
            copy.wait()
        for a in range(2):
            q_arrival(j, a).wait_recv()
            kv_arrival(j, a, HALO + other, 0).wait_recv()
        for delta in (2, 1):
            @pl.when(have(-delta))
            def _(delta=delta):
                for c in range(2):
                    for a in range(2):
                        kv_arrival(j, a, HALO - 2 * delta + c, 0).wait_recv()
        for b in range(2):
            k = kv[j, 0, b * tok:b * tok + span]
            v = kv[j, 1, b * tok:b * tok + span]
            q = jnp.concatenate([qd[j, 0, b, :, g * DH:(g + 1) * DH] for g in range(GROUP)], axis=0)
            do = jnp.concatenate([qd[j, 1, b, :, g * DH:(g + 1) * DH] for g in range(GROUP)], axis=0)
            dqs = []
            dk = dv = None
            for c in range(GROUP * tok // CHUNK):
                cut = slice(c * CHUNK, (c + 1) * CHUNK)
                dq, dk1, dv1 = tile_grads(k, v, q[cut], do[cut], bias[b, :, cut])
                dqs.append(dq.astype(jnp.bfloat16))
                dk = dk1 if dk is None else dk + dk1
                dv = dv1 if dv is None else dv + dv1
            dq = jnp.concatenate(dqs, axis=0)
            for g in range(GROUP):
                dqb[j, b, :, g * DH:(g + 1) * DH] = dq[g * tok:(g + 1) * tok]
            if b == 0:
                acc_k[...] = dk
                acc_v[...] = dv
            else:
                for a, (acc, new) in enumerate(((acc_k, dk), (acc_v, dv))):
                    part[j, a, 0:tok] = acc[0:tok].astype(jnp.bfloat16)
                    part[j, a, tok:span] = (acc[tok:span] + new[0:span - tok]).astype(jnp.bfloat16)
                    part[j, a, span:span + tok] = new[span - tok:span].astype(jnp.bfloat16)
        for block in range(HALO):
            @pl.when(have(block // 2 - HALO // 2))
            def _(block=block):
                ret_copy(j, block).start()
        peer_copy(j).start()
        dq_copy(j).start()
        dq_keep(j).start()

    @pl.loop(0, heads)
    def _(j):
        for delta in (1, 2):
            @pl.when(have(delta))
            def _(delta=delta):
                for c in range(2):
                    ret_arrival(j, delta, c).wait_recv()
        remote(part.at[j, :, 0:tok], peer.at[j], ret_send.at[j, HALO], peer_recv.at[j], mate).wait_recv()
        for a, out in enumerate((dk_out, dv_out)):
            mine = part[j, a, rows(HALO + core)].astype(jnp.float32)
            mine = mine + back[0, core, j, a].astype(jnp.float32) + back[1, core, j, a].astype(jnp.float32)
            out[:, cols(core, j, DH)] = mine.astype(jnp.bfloat16)
            his = peer[j, a].astype(jnp.float32)
            his = his + back[0, other, j, a].astype(jnp.float32) + back[1, other, j, a].astype(jnp.float32)
            out[:, cols(other, j, DH)] = his.astype(jnp.bfloat16)

    @pl.loop(0, heads)
    def _(j):
        for delta in (2, 1):
            @pl.when(have(delta))
            def _(delta=delta):
                for c in range(2):
                    for a in range(2):
                        kv_copy(j, a, delta, c).wait_send()
        for a in range(2):
            kv_copy(j, a, 0, other).wait_send()
            q_copy(j, a).wait_send()
        for block in range(HALO):
            @pl.when(have(block // 2 - HALO // 2))
            def _(block=block):
                ret_copy(j, block).wait_send()
        peer_copy(j).wait_send()
        dq_copy(j).wait_send()
        dq_arrival(j).wait_recv()
        dq_keep(j).wait()


def per_device(queries, keys, values, grad_out, positions, segments):
    tok = queries.shape[0]
    n = lax.axis_size("ctx")
    heads = HK // 2
    wide = GROUP * DH
    span = (HALO + 1) * tok
    code = positions + segments * SHIFT
    code = jnp.concatenate([jnp.full((HALO * tok,), -(1 << 30), jnp.int32), code])[None, :]
    bf = jnp.bfloat16
    dma = pltpu.SemaphoreType.DMA
    anywhere = pl.BlockSpec(memory_space=pl.ANY)
    vmem = pl.BlockSpec(memory_space=pltpu.VMEM)
    return pl.pallas_call(
        functools.partial(kernel, n),
        in_specs=[anywhere] * 4 + [vmem],
        out_specs=[anywhere, vmem, vmem],
        out_shape=[
            jax.ShapeDtypeStruct(queries.shape, bf),
            jax.ShapeDtypeStruct(keys.shape, bf),
            jax.ShapeDtypeStruct(values.shape, bf),
        ],
        scratch_shapes=[
            pltpu.VMEM((heads, 2, 2, tok, wide), bf),
            pltpu.VMEM((heads, 2, span + tok, DH), bf),
            pltpu.VMEM((heads, 2, tok, wide), bf),
            pltpu.VMEM((heads, 2, span + tok, DH), bf),
            pltpu.VMEM((2, 2, heads, 2, tok, DH), bf),
            pltpu.VMEM((heads, 2, tok, DH), bf),
            pltpu.VMEM((span, DH), jnp.float32),
            pltpu.VMEM((span, DH), jnp.float32),
            pltpu.VMEM((2, span, GROUP * tok), jnp.float32),
            dma((heads, 4)),
            dma((heads, 2)),
            dma((heads, 2)),
            dma((heads, 2, HALO + 2)),
            dma((heads, 2, HALO + 2)),
            dma((heads, 3)),
            dma((heads, HALO + 1)),
            dma((heads, 2, 2)),
            dma((heads,)),
        ],
        compiler_params=pltpu.CompilerParams(
            vmem_limit_bytes=56 * 1024 * 1024, collective_id=0, has_side_effects=True
        ),
    )(queries, grad_out, keys, values, code)


def solution(mesh):
    rows = P(("groups", "ctx"), None)
    return jax.shard_map(
        per_device,
        mesh=mesh,
        in_specs=(rows, rows, rows, rows, P("groups"), P("groups")),
        out_specs=(rows, rows, rows),
        check_vma=False,
    )
```

```python
import functools

import jax
import jax.numpy as jnp
from jax import lax
from jax.experimental import pallas as pl
from jax.experimental.pallas import tpu as pltpu
from jax.sharding import PartitionSpec as P

HQ = 32
HK = 8
DH = 128
GROUP = HQ // HK
WINDOW = 768
HALO = 4
SCALE = float(DH) ** (-0.5)
LOG2E = 1.4426950408889634
NEG = -1e30
SHIFT = 1 << 20
CHUNK = 256
NT = (((1,), (1,)), ((), ()))
TN = (((0,), (0,)), ((), ()))
NN = (((1,), (0,)), ((), ()))


def dot(a, b, dims):
    return lax.dot_general(a, b, dims, preferred_element_type=jnp.float32)


def tile_grads(k, v, q, do, bias):
    s = dot(k, q, NT) + bias
    dp = dot(v, do, NT)
    m = jnp.max(s, axis=0, keepdims=True)
    e = jnp.exp2((s - m) * (SCALE * LOG2E))
    inv = 1.0 / jnp.sum(e, axis=0, keepdims=True)
    delta = jnp.sum(e * dp, axis=0, keepdims=True) * inv
    p = (e * inv).astype(jnp.bfloat16)
    a = inv * SCALE
    ds = (e * (dp * a - delta * a)).astype(jnp.bfloat16)
    dv = dot(p, do, NN)
    dk = dot(ds, q, NN)
    dq = dot(ds, k, TN)
    return dq, dk, dv


def remote(src, dst, send, recv, device):
    return pltpu.make_async_remote_copy(
        src_ref=src,
        dst_ref=dst,
        send_sem=send,
        recv_sem=recv,
        device_id={"ctx": device},
        device_id_type=pl.DeviceIdType.MESH,
    )


def kernel(
    n, q_in, do_in, k_in, v_in, code_ref,
    dq_out, dk_out, dv_out,
    qd, kv, dqb, part, back, peer, acc_k, acc_v, bias,
    loc_sem, qd_send, qd_recv, kv_send, kv_recv, dq_sem, ret_send, ret_recv, peer_recv,
):
    tok = q_in.shape[0]
    heads = HK // 2
    wide = GROUP * DH
    span = (HALO + 1) * tok
    me = lax.axis_index("ctx")
    core = lax.rem(me, 2)
    chip = me // 2
    chips = n // 2
    mate = me + 1 - 2 * core
    other = 1 - core
    sides = (-2, -1, 1, 2)

    def dev(delta, c):
        return (chip + delta) * 2 + c

    def have(delta):
        return (chip + delta >= 0) & (chip + delta < chips)

    def cols(base, j, width):
        return pl.ds(pl.multiple_of((base * heads + j) * width, width), width)

    def rows(block):
        return pl.ds(pl.multiple_of(block * tok, 64), tok)

    barrier = pltpu.get_barrier_semaphore()
    pl.semaphore_signal(barrier, inc=1, device_id={"ctx": mate}, device_id_type=pl.DeviceIdType.MESH)
    for delta in sides:
        @pl.when(have(delta))
        def _(delta=delta):
            for c in range(2):
                pl.semaphore_signal(
                    barrier, inc=1, device_id={"ctx": dev(delta, c)}, device_id_type=pl.DeviceIdType.MESH
                )
    amount = 1 + 2 * (jnp.minimum(chip, 2) + jnp.minimum(chips - 1 - chip, 2))
    pl.semaphore_wait(barrier, amount)

    srcs = ((q_in, do_in), (k_in, v_in))

    def local_copies(j):
        out = []
        for a in range(2):
            out.append(pltpu.make_async_copy(
                srcs[0][a].at[:, cols(core, j, wide)], qd.at[j, a, core], loc_sem.at[j, a]))
            out.append(pltpu.make_async_copy(
                srcs[1][a].at[:, cols(core, j, DH)], kv.at[j, a, rows(HALO + core)], loc_sem.at[j, 2 + a]))
        return out

    def q_copy(j, a):
        return remote(srcs[0][a].at[:, cols(other, j, wide)], qd.at[j, a, core],
                      qd_send.at[j, a], qd_recv.at[j, a], mate)

    def q_arrival(j, a):
        return remote(srcs[0][a].at[:, cols(other, j, wide)], qd.at[j, a, other],
                      qd_send.at[j, a], qd_recv.at[j, a], mate)

    def kv_copy(j, a, delta, c):
        return remote(srcs[1][a].at[:, cols(c, j, DH)], kv.at[j, a, rows(HALO - 2 * delta + core)],
                      kv_send.at[j, a, 2 * delta + c], kv_recv.at[j, a, HALO - 2 * delta + core], dev(delta, c))

    def kv_arrival(j, a, block, c):
        return remote(srcs[1][a].at[:, cols(core, j, DH)], kv.at[j, a, rows(block)],
                      kv_send.at[j, a, 0], kv_recv.at[j, a, block], mate)

    @pl.loop(0, heads)
    def _(j):
        for delta in (2, 1):
            @pl.when(have(delta))
            def _(delta=delta):
                for c in range(2):
                    for a in range(2):
                        kv_copy(j, a, delta, c).start()
        for a in range(2):
            kv_copy(j, a, 0, other).start()
            q_copy(j, a).start()
        for copy in local_copies(j):
            copy.start()

    for delta in (1, 2):
        @pl.when(jnp.logical_not(have(-delta)))
        def _(delta=delta):
            lo = (HALO - 2 * delta) * tok
            kv[:, :, lo:lo + 2 * tok, :] = jnp.zeros((heads, 2, 2 * tok, DH), kv.dtype)

        @pl.when(jnp.logical_not(have(delta)))
        def _(delta=delta):
            back[delta - 1] = jnp.zeros(back.shape[1:], back.dtype)

    start = pl.multiple_of(chip * (2 * tok), 128)
    code = code_ref[:, pl.ds(start, span + tok)]
    column = jnp.broadcast_to(code, (8, span + tok)).T[:, 0:1]
    for b in range(2):
        lo = (HALO + b) * tok
        row = jnp.concatenate([code[:, lo:lo + tok]] * GROUP, axis=1)
        gap = row - column[b * tok:b * tok + span]
        bias[b] = jnp.where((gap >= 0) & (gap < WINDOW), 0.0, NEG).astype(jnp.float32)

    def ret_copy(j, block):
        delta = HALO // 2 - block // 2
        return remote(part.at[j, :, block * tok:(block + 1) * tok], back.at[delta - 1, core, j],
                      ret_send.at[j, block], ret_recv.at[j, delta - 1, core], dev(-delta, block % 2))

    def ret_arrival(j, delta, c):
        return remote(part.at[j, :, 0:tok], back.at[delta - 1, c, j],
                      ret_send.at[j, 0], ret_recv.at[j, delta - 1, c], mate)

    def peer_copy(j):
        return remote(part.at[j, :, rows(HALO + other)], peer.at[j],
                      ret_send.at[j, HALO], peer_recv.at[j], mate)

    def dq_copy(j):
        return remote(dqb.at[j, other], dq_out.at[:, cols(core, j, wide)],
                      dq_sem.at[j, 0], dq_sem.at[j, 1], mate)

    def dq_arrival(j):
        return remote(dqb.at[j, other], dq_out.at[:, cols(other, j, wide)],
                      dq_sem.at[j, 0], dq_sem.at[j, 1], mate)

    def dq_keep(j):
        return pltpu.make_async_copy(dqb.at[j, core], dq_out.at[:, cols(core, j, wide)], dq_sem.at[j, 2])

    @pl.loop(0, heads)
    def _(j):
        for copy in local_copies(j):
            copy.wait()
        for a in range(2):
            q_arrival(j, a).wait_recv()
            kv_arrival(j, a, HALO + other, 0).wait_recv()
        for delta in (2, 1):
            @pl.when(have(-delta))
            def _(delta=delta):
                for c in range(2):
                    for a in range(2):
                        kv_arrival(j, a, HALO - 2 * delta + c, 0).wait_recv()
        for b in range(2):
            k = kv[j, 0, b * tok:b * tok + span]
            v = kv[j, 1, b * tok:b * tok + span]
            q = jnp.concatenate([qd[j, 0, b, :, g * DH:(g + 1) * DH] for g in range(GROUP)], axis=0)
            do = jnp.concatenate([qd[j, 1, b, :, g * DH:(g + 1) * DH] for g in range(GROUP)], axis=0)
            dqs = []
            dk = dv = None
            for c in range(GROUP * tok // CHUNK):
                cut = slice(c * CHUNK, (c + 1) * CHUNK)
                dq, dk1, dv1 = tile_grads(k, v, q[cut], do[cut], bias[b, :, cut])
                dqs.append(dq.astype(jnp.bfloat16))
                dk = dk1 if dk is None else dk + dk1
                dv = dv1 if dv is None else dv + dv1
            dq = jnp.concatenate(dqs, axis=0)
            for g in range(GROUP):
                dqb[j, b, :, g * DH:(g + 1) * DH] = dq[g * tok:(g + 1) * tok]
            if b == 0:
                acc_k[...] = dk
                acc_v[...] = dv
                part[j, 0, 0:tok] = dk[0:tok].astype(jnp.bfloat16)
                part[j, 1, 0:tok] = dv[0:tok].astype(jnp.bfloat16)

                @pl.when(have(-2))
                def _():
                    ret_copy(j, 0).start()
            else:
                for a, (acc, new) in enumerate(((acc_k, dk), (acc_v, dv))):
                    part[j, a, tok:span] = (acc[tok:span] + new[0:span - tok]).astype(jnp.bfloat16)
                    part[j, a, span:span + tok] = new[span - tok:span].astype(jnp.bfloat16)
        for block in range(1, HALO):
            @pl.when(have(block // 2 - HALO // 2))
            def _(block=block):
                ret_copy(j, block).start()
        peer_copy(j).start()
        dq_copy(j).start()
        dq_keep(j).start()

    @pl.loop(0, heads)
    def _(j):
        for delta in (1, 2):
            @pl.when(have(delta))
            def _(delta=delta):
                for c in range(2):
                    ret_arrival(j, delta, c).wait_recv()
        remote(part.at[j, :, 0:tok], peer.at[j], ret_send.at[j, HALO], peer_recv.at[j], mate).wait_recv()
        for a, out in enumerate((dk_out, dv_out)):
            mine = part[j, a, rows(HALO + core)].astype(jnp.float32)
            mine = mine + back[0, core, j, a].astype(jnp.float32) + back[1, core, j, a].astype(jnp.float32)
            out[:, cols(core, j, DH)] = mine.astype(jnp.bfloat16)
            his = peer[j, a].astype(jnp.float32)
            his = his + back[0, other, j, a].astype(jnp.float32) + back[1, other, j, a].astype(jnp.float32)
            out[:, cols(other, j, DH)] = his.astype(jnp.bfloat16)

    @pl.loop(0, heads)
    def _(j):
        for delta in (2, 1):
            @pl.when(have(delta))
            def _(delta=delta):
                for c in range(2):
                    for a in range(2):
                        kv_copy(j, a, delta, c).wait_send()
        for a in range(2):
            kv_copy(j, a, 0, other).wait_send()
            q_copy(j, a).wait_send()
        for block in range(HALO):
            @pl.when(have(block // 2 - HALO // 2))
            def _(block=block):
                ret_copy(j, block).wait_send()
        peer_copy(j).wait_send()
        dq_copy(j).wait_send()
        dq_arrival(j).wait_recv()
        dq_keep(j).wait()


def settle(*refs):
    count = len(refs) // 2
    for a in range(count):
        refs[count + a][...] = refs[a][...]


def per_device(queries, keys, values, grad_out, positions, segments):
    tok = queries.shape[0]
    n = lax.axis_size("ctx")
    heads = HK // 2
    wide = GROUP * DH
    span = (HALO + 1) * tok
    code = positions + segments * SHIFT
    code = jnp.concatenate([jnp.full((HALO * tok,), -(1 << 30), jnp.int32), code])[None, :]
    bf = jnp.bfloat16
    dma = pltpu.SemaphoreType.DMA
    anywhere = pl.BlockSpec(memory_space=pl.ANY)
    vmem = pl.BlockSpec(memory_space=pltpu.VMEM)
    grads = pl.pallas_call(
        functools.partial(kernel, n),
        in_specs=[anywhere] * 4 + [vmem],
        out_specs=[anywhere, vmem, vmem],
        out_shape=[
            jax.ShapeDtypeStruct(queries.shape, bf),
            jax.ShapeDtypeStruct(keys.shape, bf),
            jax.ShapeDtypeStruct(values.shape, bf),
        ],
        scratch_shapes=[
            pltpu.VMEM((heads, 2, 2, tok, wide), bf),
            pltpu.VMEM((heads, 2, span + tok, DH), bf),
            pltpu.VMEM((heads, 2, tok, wide), bf),
            pltpu.VMEM((heads, 2, span + tok, DH), bf),
            pltpu.VMEM((2, 2, heads, 2, tok, DH), bf),
            pltpu.VMEM((heads, 2, tok, DH), bf),
            pltpu.VMEM((span, DH), jnp.float32),
            pltpu.VMEM((span, DH), jnp.float32),
            pltpu.VMEM((2, span, GROUP * tok), jnp.float32),
            dma((heads, 4)),
            dma((heads, 2)),
            dma((heads, 2)),
            dma((heads, 2, HALO + 2)),
            dma((heads, 2, HALO + 2)),
            dma((heads, 3)),
            dma((heads, HALO + 1)),
            dma((heads, 2, 2)),
            dma((heads,)),
        ],
        compiler_params=pltpu.CompilerParams(
            vmem_limit_bytes=56 * 1024 * 1024, collective_id=0, has_side_effects=True
        ),
    )(queries, grad_out, keys, values, code)
    blocks = [pl.BlockSpec((tok // 4, g.shape[1]), lambda i: (i, 0)) for g in grads]
    return pl.pallas_call(
        settle,
        grid=(4,),
        in_specs=blocks,
        out_specs=blocks,
        out_shape=[jax.ShapeDtypeStruct(g.shape, g.dtype) for g in grads],
        compiler_params=pltpu.CompilerParams(vmem_limit_bytes=60 * 1024 * 1024),
    )(*grads)


def solution(mesh):
    rows = P(("groups", "ctx"), None)
    return jax.shard_map(
        per_device,
        mesh=mesh,
        in_specs=(rows, rows, rows, rows, P("groups"), P("groups")),
        out_specs=(rows, rows, rows),
        check_vma=False,
    )
```
